32 devices in a mesh: row: 8 (over y, x, core), col: 4 (over z).
Axes of the slice: x: 2, y: 2, z: 4, core: 2. Of those that a mesh axis runs over, the one named last changes fastest.
Arguments:
- gate_feats: bfloat16 [8, 4, 1024, 256], P('row', 'col'), may hold values from -6 to 6
- adjacency: int32 [8, 4, 8, 5, 128, 128], P('row', 'col'), may hold values 0 or 1
- gate_count: int32 [8, 4], P('row', 'col'), may hold values from 128 to 1024, as said below
- membership: int32 [8, 4, 512, 1024], P('row', 'col'), may hold values 0 or 1
- tok_count: int32 [8, 4], P('row', 'col'), may hold values from 64 to 512, as said below
- w_msg: bfloat16 [256, 256], replicated, may hold values from -0.375 to 0.375
- w_query: bfloat16 [256, 256], replicated, may hold values from -0.375 to 0.375
- w_key: bfloat16 [256, 256], replicated, may hold values from -0.375 to 0.375
- w_value: bfloat16 [256, 256], replicated, may hold values from -0.375 to 0.375
- w_out: bfloat16 [256, 256], replicated, may hold values from -0.375 to 0.375
- w_score: bfloat16 [256], replicated, may hold values from -0.375 to 0.375
- cotangent: float32 [8, 4, 512], P('row', 'col'), may hold values from -6 to 6
Outputs:
- value_out: float32 [8, 4, 512], P('row', 'col')
- g_msg: float32 [256, 256], replicated
- g_query: float32 [256, 256], replicated
- g_key: float32 [256, 256], replicated
- g_value: float32 [256, 256], replicated
- g_out: float32 [256, 256], replicated
- g_score: float32 [256], replicated
The draws below stay inside these ranges and needn't reach their ends.
Inputs may be any that keep to these rules, and one draw needn't show every extreme that they name: `gate_count`: some tile is full in every draw. `tok_count`: some tile is full in every draw.
All inputs are finite; a program needn't handle non-finite values. No bound on the sum of `adjacency` or of `membership` on one device may be relied on, other than what follows from the above.
Results may differ from the reference program's by a relative error of at most 0.017.
Values may be sent and summed in bfloat16 or wider, within the bound.
A program may use at most 128 MiB of HBM per device.

```python
import math
import jax
import jax.numpy as jnp
from jax import lax

H = 256
HEADS = 2
HD = 128
BLK = 128
NB = 8
NT = 512
G = 1024
TROWS = 8
TCOLS = 4


def full_counts(key, most):
    counts = jax.random.randint(key, (TROWS * TCOLS,), most // 8, most + 1)
    chosen = jax.random.randint(jax.random.fold_in(key, 7), (), 0, TROWS * TCOLS)
    counts = counts.at[chosen].set(most)
    return counts.reshape(TROWS, TCOLS).astype(jnp.int32)


def draw_gate_count(key, part):
    return full_counts(jax.random.fold_in(key, 11), G)


def draw_tok_count(key, part):
    return full_counts(jax.random.fold_in(key, 23), NT)


def with_ends(array, own_key, low, top_value):
    spot = [jax.random.randint(jax.random.fold_in(own_key, axis), (), 0, length) for axis, length in enumerate(array.shape)]
    main_axis = array.shape.index(max(array.shape))
    beside = spot[:main_axis] + [(spot[main_axis] + 1) % array.shape[main_axis]] + spot[main_axis + 1:]
    return array.at[tuple(spot)].set(low).at[tuple(beside)].set(top_value)


def levels(rng, shape, shards, low, high):
    def one(axis_at, parts):
        heights = jax.random.uniform(jax.random.fold_in(jax.random.fold_in(rng, 6), axis_at), (parts,), jnp.float32, low / len(shards), high / len(shards))
        return jnp.repeat(jnp.exp(heights), shape[axis_at] // parts).reshape((-1,) + (1,) * (len(shape) - axis_at - 1))

    factor_of = one(*shards[0])
    for cut in shards[1:]:
        factor_of = factor_of * one(*cut)
    return factor_of


def normal_values(stream_key, shape, scale, most, split=(), held_as=jnp.bfloat16):
    gain = levels(stream_key, shape, split, -0.22, 0.18) if split else 1.0
    array = jax.random.normal(stream_key, shape, jnp.float32) * scale * gain
    return jnp.minimum(jnp.maximum(array, -most), most).astype(held_as)


def setup_inputs(seed: int = 0) -> dict:
    key_of = jax.random.split(jax.random.key(seed), 13)
    gate_feats = normal_values(key_of[0], (TROWS, TCOLS, G, H), 1.0, 6.0, ((0, 8), (1, 4)))
    adjacency = with_ends((jax.random.randint(key_of[1], (TROWS, TCOLS, NB, 5, BLK, BLK), 0, 16) < 1).astype(jnp.int32), jax.random.fold_in(key_of[1], 1), 0, 1)
    gate_count = draw_gate_count(jax.random.fold_in(key_of[12], 71), 0)
    membership = with_ends((jax.random.randint(key_of[3], (TROWS, TCOLS, NT, G), 0, 32) < 1).astype(jnp.int32), jax.random.fold_in(key_of[3], 1), 0, 1)
    tok_count = draw_tok_count(jax.random.fold_in(key_of[12], 71), 0)
    w_msg = normal_values(key_of[5], (H, H), H ** -0.5, 0.375)
    w_query = normal_values(key_of[6], (H, H), H ** -0.5, 0.375)
    w_key = normal_values(key_of[7], (H, H), H ** -0.5, 0.375)
    w_value = normal_values(key_of[8], (H, H), H ** -0.5, 0.375)
    w_out = normal_values(key_of[9], (H, H), H ** -0.5, 0.375)
    w_score = normal_values(key_of[10], (H,), H ** -0.5, 0.375)
    cotangent = normal_values(key_of[11], (TROWS, TCOLS, NT), 1.0, 6.0, ((0, 8), (1, 4)), jnp.float32)
    return dict(gate_feats=gate_feats, adjacency=adjacency, gate_count=gate_count, membership=membership, tok_count=tok_count, w_msg=w_msg, w_query=w_query, w_key=w_key, w_value=w_value, w_out=w_out, w_score=w_score, cotangent=cotangent)


EPS = 1e-06

def silu_grad(preact):
    sigmoid_val = jax.nn.sigmoid(preact)
    return sigmoid_val * (1.0 + preact * (1.0 - sigmoid_val))

def rms_forward(values_in):
    rscale = lax.rsqrt(lax.optimization_barrier(jnp.mean(values_in * values_in, axis=-1, keepdims=True)) + EPS)
    return (values_in * rscale, rscale)

def rms_backward(grad_in, normed, rscale):
    return rscale * (grad_in - normed * lax.optimization_barrier(jnp.mean(grad_in * normed, axis=-1, keepdims=True)))

def split_heads(rows_in):
    return rows_in.astype(jnp.float32).reshape(rows_in.shape[0], HEADS, HD)

def score_probs(query_rows, key_rows):
    scores = jnp.einsum('qhd,khd->hqk', split_heads(query_rows), split_heads(key_rows))
    return jax.nn.sigmoid(scores / math.sqrt(HD) - math.log(NT))

def attend(query_rows, key_rows, value_rows):
    weights = lax.optimization_barrier(score_probs(query_rows, key_rows).astype(jnp.bfloat16)).astype(jnp.float32)
    output = jnp.einsum('hqk,khd->qhd', weights, split_heads(value_rows))
    return output.reshape(query_rows.shape[0], H).astype(jnp.bfloat16)

def attend_grads(query_rows, grad_rows, key_rows, value_rows):
    probs_val = score_probs(query_rows, key_rows)
    weights = lax.optimization_barrier(probs_val.astype(jnp.bfloat16)).astype(jnp.float32)
    grad_prob = jnp.einsum('qhd,khd->hqk', split_heads(grad_rows), split_heads(value_rows))
    grad_score = grad_prob * probs_val * (1.0 - probs_val) / math.sqrt(HD)
    grad_score = lax.optimization_barrier(grad_score.astype(jnp.bfloat16)).astype(jnp.float32)
    grad_query = jnp.einsum('hqk,khd->qhd', grad_score, split_heads(key_rows)).reshape(query_rows.shape[0], H)
    grad_key = jnp.einsum('hqk,qhd->khd', grad_score, split_heads(query_rows)).reshape(key_rows.shape[0], H)
    grad_val = jnp.einsum('hqk,qhd->khd', weights, split_heads(grad_rows)).reshape(key_rows.shape[0], H)
    return (grad_query, grad_key, grad_val)

def reference(gate_feats, adjacency, gate_count, membership, tok_count, w_msg, w_query, w_key, w_value, w_out, w_score, cotangent):
    gate_live = (jnp.arange(G)[None, None, :] < gate_count[:, :, None]).astype(jnp.float32)
    live_feats = (gate_feats.astype(jnp.float32) * gate_live[..., None]).astype(jnp.bfloat16)
    padded = jnp.pad(live_feats, ((1, 1), (1, 1), (0, 0), (0, 0)))

    def tile_row(row_idx):
        near = lax.dynamic_slice_in_dim(padded, row_idx, 3, 0)
        sources = jnp.stack([near[1, 1:-1], near[0, 1:-1], near[2, 1:-1], near[1, :-2], near[1, 2:]], axis=1)
        sources = sources.reshape(TCOLS, 5, NB, BLK, H).astype(jnp.float32)
        adj_tiles = lax.dynamic_index_in_dim(adjacency, row_idx, 0, keepdims=False).astype(jnp.float32)
        aggregate = jnp.einsum('cbkij,ckbjh->cbih', adj_tiles, sources)
        degree = lax.optimization_barrier(jnp.sum(adj_tiles, axis=(2, 4)))
        message = (aggregate / (degree[..., None] + 1.0)).astype(jnp.bfloat16).reshape(TCOLS, G, H)
        preact = jnp.dot(message, w_msg, preferred_element_type=jnp.float32)
        live_row = lax.dynamic_index_in_dim(gate_live, row_idx, 0, keepdims=False)
        feat_row = lax.dynamic_index_in_dim(live_feats, row_idx, 0, keepdims=False)
        hidden = (live_row[..., None] * (feat_row.astype(jnp.float32) + jax.nn.silu(preact))).astype(jnp.bfloat16)
        member_rows = lax.dynamic_index_in_dim(membership, row_idx, 0, keepdims=False).astype(jnp.float32)
        member_count = lax.optimization_barrier(jnp.sum(member_rows, axis=-1, keepdims=True))
        pooled = jnp.einsum('cng,cgh->cnh', member_rows, hidden.astype(jnp.float32)) / (member_count + 1.0)
        return (message, preact, pooled, member_count)
    message, preact, pooled, member_count = lax.map(tile_row, jnp.arange(TROWS))
    normed, rscale = rms_forward(pooled)
    token_live = (jnp.arange(NT)[None, None, :] < tok_count[:, :, None]).astype(jnp.float32)
    tokens = (token_live[..., None] * normed).astype(jnp.bfloat16)
    query = jnp.dot(tokens, w_query, preferred_element_type=jnp.float32).astype(jnp.bfloat16)
    key = jnp.dot(tokens, w_key, preferred_element_type=jnp.float32).astype(jnp.bfloat16)
    value = jnp.dot(tokens, w_value, preferred_element_type=jnp.float32).astype(jnp.bfloat16)

    def attend_row(row_idx):
        key_all = lax.dynamic_index_in_dim(key, row_idx, 0, keepdims=False).reshape(TCOLS * NT, H)
        value_all = lax.dynamic_index_in_dim(value, row_idx, 0, keepdims=False).reshape(TCOLS * NT, H)
        query_row = lax.dynamic_index_in_dim(query, row_idx, 0, keepdims=False)
        return lax.map(lambda query_rows: attend(query_rows, key_all, value_all), query_row)
    attended = lax.map(attend_row, jnp.arange(TROWS))
    proj = jnp.dot(attended, w_out, preferred_element_type=jnp.float32)
    pnormed, pscale = rms_forward(proj)
    mixed = tokens.astype(jnp.float32) + pnormed
    score_w = w_score.astype(jnp.float32)
    value_out = token_live * lax.optimization_barrier(jnp.sum(mixed * score_w, axis=-1))
    grad_value = token_live * cotangent / math.sqrt(TROWS * TCOLS * NT)
    g_score = jnp.einsum('rcn,rcnh->h', grad_value, mixed)
    grad_mixed = grad_value[..., None] * score_w
    grad_proj = rms_backward(grad_mixed, pnormed, pscale).astype(jnp.bfloat16)
    g_out = jnp.einsum('rcnh,rcne->he', attended.astype(jnp.float32), grad_proj.astype(jnp.float32))
    grad_attn = jnp.dot(grad_proj, w_out.T, preferred_element_type=jnp.float32).astype(jnp.bfloat16)

    def grads_row(row_idx):
        key_all = lax.dynamic_index_in_dim(key, row_idx, 0, keepdims=False).reshape(TCOLS * NT, H)
        value_all = lax.dynamic_index_in_dim(value, row_idx, 0, keepdims=False).reshape(TCOLS * NT, H)
        query_row = lax.dynamic_index_in_dim(query, row_idx, 0, keepdims=False)
        grad_row = lax.dynamic_index_in_dim(grad_attn, row_idx, 0, keepdims=False)

        def per_tile(totals, tile_pair):
            grad_q, grad_k, grad_v = attend_grads(tile_pair[0], tile_pair[1], key_all, value_all)
            return ((totals[0] + grad_k, totals[1] + grad_v), grad_q)
        zero_rows = jnp.zeros((TCOLS * NT, H), jnp.float32)
        sums, grad_q_row = lax.scan(per_tile, (zero_rows, zero_rows), (query_row, grad_row))
        return (grad_q_row, sums[0].reshape(TCOLS, NT, H), sums[1].reshape(TCOLS, NT, H))
    grad_query, grad_key, grad_val = lax.map(grads_row, jnp.arange(TROWS))
    grad_query = grad_query.astype(jnp.bfloat16)
    grad_key = grad_key.astype(jnp.bfloat16)
    grad_val = grad_val.astype(jnp.bfloat16)
    tokens_f = tokens.astype(jnp.float32)
    g_query = jnp.einsum('rcnh,rcne->he', tokens_f, grad_query.astype(jnp.float32))
    g_key = jnp.einsum('rcnh,rcne->he', tokens_f, grad_key.astype(jnp.float32))
    g_value = jnp.einsum('rcnh,rcne->he', tokens_f, grad_val.astype(jnp.float32))
    grad_tokens = grad_mixed + jnp.dot(grad_query, w_query.T, preferred_element_type=jnp.float32)
    grad_tokens = grad_tokens + jnp.dot(grad_key, w_key.T, preferred_element_type=jnp.float32)
    grad_tokens = grad_tokens + jnp.dot(grad_val, w_value.T, preferred_element_type=jnp.float32)
    grad_pooled = rms_backward(token_live[..., None] * grad_tokens, normed, rscale)
    grad_scaled = (grad_pooled / (member_count + 1.0)).astype(jnp.bfloat16)

    def msg_row(row_idx):
        member_rows = lax.dynamic_index_in_dim(membership, row_idx, 0, keepdims=False).astype(jnp.float32)
        scaled_row = lax.dynamic_index_in_dim(grad_scaled, row_idx, 0, keepdims=False).astype(jnp.float32)
        grad_hidden = jnp.einsum('cng,cnh->cgh', member_rows, scaled_row)
        live_row = lax.dynamic_index_in_dim(gate_live, row_idx, 0, keepdims=False)
        pre_row = lax.dynamic_index_in_dim(preact, row_idx, 0, keepdims=False)
        grad_pre = (live_row[..., None] * grad_hidden * silu_grad(pre_row)).astype(jnp.bfloat16)
        msg_row_vals = lax.dynamic_index_in_dim(message, row_idx, 0, keepdims=False)
        return jnp.einsum('cgh,cge->he', msg_row_vals.astype(jnp.float32), grad_pre.astype(jnp.float32))
    g_msg = lax.optimization_barrier(jnp.sum(lax.map(msg_row, jnp.arange(TROWS)), axis=0))
    return (value_out, g_msg, g_query, g_key, g_value, g_out, g_score)
```

```python
import math

import jax
import jax.numpy as jnp
from jax import lax
from jax.experimental import pallas as pl
from jax.experimental.pallas import tpu as pltpu
from jax.sharding import PartitionSpec as P

H = 256
HEADS = 2
HD = 128
BLK = 128
NB = 8
NT = 512
G = NB * BLK
NCH = 4
CG = G // NCH
EPS = 1e-06
F32 = jnp.float32
BF16 = jnp.bfloat16
MESH = pl.DeviceIdType.MESH


def mm(a, b):
    return jnp.dot(a, b, preferred_element_type=F32)


def mm_nt(a, b):
    return lax.dot_general(a, b, (((1,), (1,)), ((), ())), preferred_element_type=F32)


def mm_tn(a, b):
    return lax.dot_general(a, b, (((0,), (0,)), ((), ())), preferred_element_type=F32)


def remote(src, dst, send, recv, axis, peer):
    return pltpu.make_async_remote_copy(
        src_ref=src, dst_ref=dst, send_sem=send, recv_sem=recv,
        device_id={axis: peer}, device_id_type=MESH,
    )


def others(size, func):
    def step(s, carry):
        func(s)
        return carry

    lax.fori_loop(1, size, step, 0)


def rms_forward(values_in):
    rscale = lax.rsqrt(jnp.mean(values_in * values_in, axis=-1, keepdims=True) + EPS)
    return (values_in * rscale, rscale)


def rms_backward(grad_in, normed, rscale):
    return rscale * (grad_in - normed * jnp.mean(grad_in * normed, axis=-1, keepdims=True))


def prob_parts(scores):
    expo = math.log2(NT) - scores * (math.log2(math.e) / math.sqrt(HD))
    power = jnp.exp2(jnp.minimum(expo, 120.0))
    prob = pl.reciprocal(1.0 + power, approx=True)
    return prob, prob * (prob * power) * (1.0 / math.sqrt(HD))


def kernel(
    rows, cols,
    gate_count, tok_count, feats_hbm, adj_hbm, mem_hbm,
    w_msg, w_query, w_key, w_value, w_out, w_score, cot,
    value_out, g_msg, g_query, g_key, g_value, g_out, g_score,
    feats, live, halo, adj_i, mem_i, adj, inv_deg, mem, mem_t, inv_cnt,
    message, preact, pooled, normed, rscale,
    tok, q_all, k_all, v_all, ga_all, d_own, p_t, d_t, att, gq, gk, gv, gmix,
    sa, ra, sb, rb, sc, rc, ta, ua, tb, ub, tc, uc, fa, fb, fc,
    local_sem, halo_s, halo_r, tok_s, tok_r, ga_s, ga_r,
    one_s, one_r, two_s, two_r, three_s, three_r,
):
    r = lax.axis_index("row")
    c = lax.axis_index("col")
    ch = H // rows

    load_feats = pltpu.make_async_copy(feats_hbm, feats, local_sem.at[0])
    load_adj = pltpu.make_async_copy(adj_hbm, adj_i, local_sem.at[1])
    load_mem = pltpu.make_async_copy(mem_hbm, mem_i, local_sem.at[2])
    load_feats.start()
    load_adj.start()
    load_mem.start()

    barrier = pltpu.get_barrier_semaphore()
    others(rows, lambda s: pl.semaphore_signal(
        barrier, inc=1, device_id={"row": lax.rem(r + s, rows)}, device_id_type=MESH))
    others(cols, lambda s: pl.semaphore_signal(
        barrier, inc=1, device_id={"col": lax.rem(c + s, cols)}, device_id_type=MESH))

    gates = gate_count[0, 0]
    load_feats.wait()
    for i in range(NCH):
        alive = (lax.broadcasted_iota(jnp.int32, (CG, 1), 0) + i * CG < gates).astype(F32)
        live[i] = (feats[i * CG:(i + 1) * CG].astype(F32) * alive).astype(BF16)
    pl.semaphore_wait(barrier, rows + cols - 2)

    ways = (
        (2, "col", 1, c < cols - 1, c > 0),
        (3, "col", -1, c > 0, c < cols - 1),
        (0, "row", 1, r < rows - 1, r > 0),
        (1, "row", -1, r > 0, r < rows - 1),
    )
    place = {"row": r, "col": c}

    def halo_copy(way, i):
        slot, axis, step, _, _ = way
        return remote(live.at[i], halo.at[slot, i], halo_s.at[slot, i], halo_r.at[slot, i],
                      axis, place[axis] + step)

    for way in ways:
        @pl.when(jnp.logical_not(way[4]))
        def _(way=way):
            halo[way[0]] = jnp.zeros((NCH, CG, H), BF16)

        @pl.when(way[3])
        def _(way=way):
            for i in range(NCH):
                halo_copy(way, i).start()

    load_adj.wait()

    def adj_step(b, carry):
        parts = [adj_i[b, k].astype(F32) for k in range(5)]
        total = parts[0] + parts[1] + parts[2] + parts[3] + parts[4]
        inv_deg[b] = 1.0 / (jnp.sum(total, axis=1, keepdims=True) + 1.0)
        for k in range(5):
            adj[b, :, k * BLK:(k + 1) * BLK] = parts[k].astype(BF16)
        return carry

    lax.fori_loop(0, NB, adj_step, 0)
    load_mem.wait()
    count = jnp.zeros((NT, 1), F32)
    for i in range(NCH):
        part = mem_i[:, i * CG:(i + 1) * CG].astype(F32)
        count = count + jnp.sum(part, axis=1, keepdims=True)
        mem[i] = part.astype(BF16)
        mem_t[i] = part.T.astype(BF16)
    inv_cnt[...] = 1.0 / (count + 1.0)

    pooled[...] = jnp.zeros((NT, H), F32)

    def gate_step(i, carry):
        for way in ways:
            @pl.when(way[4])
            def _(way=way):
                slot, axis, step, _, _ = way
                remote(live.at[i], halo.at[slot, i], halo_s.at[slot, i], halo_r.at[slot, i],
                       axis, place[axis] - step).wait_recv()
        own = live[i]
        for b in range(CG // BLK):
            cut = slice(b * BLK, (b + 1) * BLK)
            blk = i * (CG // BLK) + b
            srcs = jnp.concatenate([own[cut]] + [halo[k, i, cut] for k in range(4)], axis=0)
            message[i, cut] = (mm(adj[blk], srcs) * inv_deg[blk]).astype(BF16)
        pre = mm(message[i], w_msg[...])
        preact[i] = pre
        alive = (lax.broadcasted_iota(jnp.int32, (CG, 1), 0) + i * CG < gates).astype(F32)
        hidden = (alive * (own.astype(F32) + pre / (1.0 + jnp.exp(-pre)))).astype(BF16)
        pooled[...] += mm(mem[i], hidden)
        return carry

    lax.fori_loop(0, NCH, gate_step, 0)

    n_live = tok_count[0, 0]
    tlive = (lax.broadcasted_iota(jnp.int32, (NT, 1), 0) < n_live).astype(F32)
    norm_val, rs_val = rms_forward(pooled[...] * inv_cnt[...])
    normed[...] = norm_val
    rscale[...] = rs_val
    tok[c] = (tlive * norm_val).astype(BF16)

    def tok_copy(peer, slot):
        return remote(tok.at[slot], tok.at[slot], tok_s.at[peer], tok_r.at[slot], "col", peer)

    others(cols, lambda s: tok_copy(lax.rem(c + s, cols), c).start())
    own_tok = tok[c]
    q_all[c] = mm(own_tok, w_query[...]).astype(BF16)
    att[...] = jnp.zeros((NT, H), F32)

    def attend_step(s, carry):
        src = lax.rem(c + s, cols)

        @pl.when(s > 0)
        def _():
            tok_copy(src, src).wait_recv()

        k_all[src] = mm(tok[src], w_key[...]).astype(BF16)
        v_all[src] = mm(tok[src], w_value[...]).astype(BF16)
        for h in range(HEADS):
            lanes = slice(h * HD, (h + 1) * HD)
            prob, slope = prob_parts(mm_nt(q_all[c, :, lanes], k_all[src, :, lanes]))
            d_own[src, h] = slope.astype(BF16)
            att[:, lanes] += mm(prob.astype(BF16), v_all[src, :, lanes])
        return carry

    lax.fori_loop(0, cols, attend_step, 0)

    attended = att[...].astype(BF16)
    pnormed, pscale = rms_forward(mm(attended, w_out[...]))
    mixed = own_tok.astype(F32) + pnormed
    score_w = w_score[...].astype(F32)
    val = tlive * jnp.sum(mixed * score_w, axis=1, keepdims=True)
    value_out[...] = jnp.broadcast_to(val, (NT, 128)).T[0:1]
    cot_col = jnp.broadcast_to(cot[...], (128, NT)).T[:, 0:1]
    grad_value = tlive * cot_col * (1.0 / math.sqrt(rows * cols * NT))
    grad_mixed = grad_value * score_w
    gmix[...] = grad_mixed
    grad_proj = rms_backward(grad_mixed, pnormed, pscale).astype(BF16)
    ga_all[c] = mm_nt(grad_proj, w_out[...]).astype(BF16)

    def ga_copy(peer, slot):
        return remote(ga_all.at[slot], ga_all.at[slot], ga_s.at[peer], ga_r.at[slot], "col", peer)

    others(cols, lambda s: ga_copy(lax.rem(c + s, cols), c).start())

    def one_copy(g, send, recv, peer, slot):
        return remote(send.at[peer], recv.at[slot], one_s.at[g, peer], one_r.at[g, slot], "row", peer)

    def one_start(g, send, recv):
        recv[r] = send[r]
        others(rows, lambda s: one_copy(g, send, recv, lax.rem(r + s, rows), r).start())

    def two_copy(g, send, recv, peer, slot):
        return remote(send, recv.at[slot], two_s.at[g, peer], two_r.at[g, slot], "col", peer)

    def two_start(g, send, recv, mid, gathered):
        others(rows, lambda s: one_copy(
            g, send, recv, lax.rem(r + s, rows), lax.rem(r + s, rows)).wait_recv())
        total = recv[0].astype(F32)
        for p in range(1, rows):
            total = total + recv[p].astype(F32)
        mid[...] = total.astype(BF16)
        gathered[c] = mid[...]
        others(cols, lambda s: two_copy(g, mid, gathered, lax.rem(c + s, cols), c).start())

    def three_copy(g, full, peer, slot):
        return remote(full.at[slot], full.at[slot], three_s.at[g, peer], three_r.at[g, slot],
                      "row", peer)

    def three_start(g, mid, gathered, full, span):
        others(cols, lambda s: two_copy(
            g, mid, gathered, lax.rem(c + s, cols), lax.rem(c + s, cols)).wait_recv())
        total = gathered[0].astype(F32)
        for p in range(1, cols):
            total = total + gathered[p].astype(F32)
        full[r] = total[:span].astype(BF16)
        others(rows, lambda s: three_copy(g, full, lax.rem(r + s, rows), r).start())
        return total

    def three_wait(g, full):
        others(rows, lambda s: three_copy(
            g, full, lax.rem(r + s, rows), lax.rem(r + s, rows)).wait_recv())

    def finish(g, send, recv, mid, gathered, full):
        def row_send(s):
            p = lax.rem(r + s, rows)
            one_copy(g, send, recv, p, r).wait_send()
            three_copy(g, full, p, r).wait_send()

        others(rows, row_send)
        others(cols, lambda s: two_copy(g, mid, gathered, lax.rem(c + s, cols), c).wait_send())

    score_part = jnp.broadcast_to(jnp.sum(mixed * grad_value, axis=0, keepdims=True), (16, H))
    out_part = mm_tn(attended, grad_proj)
    for p in range(rows):
        sa[p, 0:ch] = out_part[p * ch:(p + 1) * ch].astype(BF16)
        sa[p, ch:ch + 16] = score_part.astype(BF16)
    one_start(0, sa, ra)

    gq[...] = jnp.zeros((NT, H), F32)
    gk[...] = jnp.zeros((NT, H), F32)
    gv[...] = jnp.zeros((NT, H), F32)

    def query_step(s, carry):
        src = lax.rem(c + s, cols)
        q_all[src] = mm(tok[src], w_query[...]).astype(BF16)
        for h in range(HEADS):
            lanes = slice(h * HD, (h + 1) * HD)
            grad_prob = mm_nt(ga_all[c, :, lanes], v_all[src, :, lanes])
            grad_score = (grad_prob * d_own[src, h].astype(F32)).astype(BF16)
            gq[:, lanes] += mm(grad_score, k_all[src, :, lanes])
            prob, slope = prob_parts(mm_nt(k_all[c, :, lanes], q_all[src, :, lanes]))
            p_t[src, h] = prob.astype(BF16)
            d_t[src, h] = slope.astype(BF16)
        return carry

    lax.fori_loop(0, cols, query_step, 0)
    two_start(0, sa, ra, ta, ua)

    def key_step(s, carry):
        src = lax.rem(c + s, cols)

        @pl.when(s > 0)
        def _():
            ga_copy(src, src).wait_recv()

        for h in range(HEADS):
            lanes = slice(h * HD, (h + 1) * HD)
            grad_prob = mm_nt(v_all[c, :, lanes], ga_all[src, :, lanes])
            grad_score = (grad_prob * d_t[src, h].astype(F32)).astype(BF16)
            gk[:, lanes] += mm(grad_score, q_all[src, :, lanes])
            gv[:, lanes] += mm(p_t[src, h], ga_all[src, :, lanes])
        return carry

    lax.fori_loop(0, cols, key_step, 0)

    grad_query = gq[...].astype(BF16)
    grad_key = gk[...].astype(BF16)
    grad_val = gv[...].astype(BF16)
    for j, grad in enumerate((grad_query, grad_key, grad_val)):
        part = mm_tn(own_tok, grad).astype(BF16)
        for p in range(rows):
            sb[p, j * ch:(j + 1) * ch] = part[p * ch:(p + 1) * ch]
    one_start(1, sb, rb)

    grad_tokens = gmix[...] + mm_nt(grad_query, w_query[...])
    grad_tokens = grad_tokens + mm_nt(grad_key, w_key[...])
    grad_tokens = grad_tokens + mm_nt(grad_val, w_value[...])
    grad_pooled = rms_backward(tlive * grad_tokens, normed[...], rscale[...])
    grad_scaled = (grad_pooled * inv_cnt[...]).astype(BF16)
    msg_part = jnp.zeros((H, H), F32)
    for i in range(NCH):
        alive = (lax.broadcasted_iota(jnp.int32, (CG, 1), 0) + i * CG < gates).astype(F32)
        pre = preact[i]
        sig = 1.0 / (1.0 + jnp.exp(-pre))
        grad_pre = alive * mm(mem_t[i], grad_scaled) * (sig * (1.0 + pre * (1.0 - sig)))
        msg_part = msg_part + mm_tn(message[i], grad_pre.astype(BF16))
    for p in range(rows):
        sc[p] = msg_part[p * ch:(p + 1) * ch].astype(BF16)
    one_start(2, sc, rc)

    two_start(1, sb, rb, tb, ub)
    total = three_start(0, ta, ua, fa, ch)
    g_score[...] = total[ch:ch + 1]
    two_start(2, sc, rc, tc, uc)
    three_start(1, tb, ub, fb, 3 * ch)
    three_start(2, tc, uc, fc, ch)
    three_wait(0, fa)
    for p in range(rows):
        g_out[p * ch:(p + 1) * ch] = fa[p].astype(F32)
    three_wait(1, fb)
    for p in range(rows):
        for j, out in enumerate((g_query, g_key, g_value)):
            out[p * ch:(p + 1) * ch] = fb[p, j * ch:(j + 1) * ch].astype(F32)
    three_wait(2, fc)
    for p in range(rows):
        g_msg[p * ch:(p + 1) * ch] = fc[p].astype(F32)

    for way in ways:
        @pl.when(way[3])
        def _(way=way):
            for i in range(NCH):
                halo_copy(way, i).wait_send()

    def col_send(s):
        p = lax.rem(c + s, cols)
        tok_copy(p, c).wait_send()
        ga_copy(p, c).wait_send()

    others(cols, col_send)
    finish(0, sa, ra, ta, ua, fa)
    finish(1, sb, rb, tb, ub, fb)
    finish(2, sc, rc, tc, uc, fc)


def solution(mesh):
    rows, cols = mesh.shape["row"], mesh.shape["col"]
    ch = H // rows

    def body(gate_feats, adjacency, gate_count, membership, tok_count,
             w_msg, w_query, w_key, w_value, w_out, w_score, cotangent):
        vmem = pl.BlockSpec(memory_space=pltpu.VMEM)
        smem = pl.BlockSpec(memory_space=pltpu.SMEM)
        hbm = pl.BlockSpec(memory_space=pl.ANY)
        wide = jax.ShapeDtypeStruct((H, H), F32)
        dma = pltpu.SemaphoreType.DMA
        V = pltpu.VMEM
        outs = pl.pallas_call(
            lambda *refs: kernel(rows, cols, *refs),
            out_shape=[jax.ShapeDtypeStruct((1, NT), F32), wide, wide, wide, wide, wide,
                       jax.ShapeDtypeStruct((1, H), F32)],
            in_specs=[smem, smem, hbm, hbm, hbm] + [vmem] * 7,
            out_specs=[vmem] * 7,
            scratch_shapes=[
                V((G, H), BF16), V((NCH, CG, H), BF16), V((4, NCH, CG, H), BF16),
                V((NB, 5, BLK, BLK), jnp.int32), V((NT, G), jnp.int32),
                V((NB, BLK, 5 * BLK), BF16), V((NB, BLK, 1), F32),
                V((NCH, NT, CG), BF16), V((NCH, CG, NT), BF16), V((NT, 1), F32),
                V((NCH, CG, H), BF16), V((NCH, CG, H), F32), V((NT, H), F32),
                V((NT, H), F32), V((NT, 1), F32),
                V((cols, NT, H), BF16), V((cols, NT, H), BF16), V((cols, NT, H), BF16),
                V((cols, NT, H), BF16), V((cols, NT, H), BF16),
                V((cols, HEADS, NT, NT), BF16), V((cols, HEADS, NT, NT), BF16),
                V((cols, HEADS, NT, NT), BF16),
                V((NT, H), F32), V((NT, H), F32), V((NT, H), F32), V((NT, H), F32),
                V((NT, H), F32),
                V((rows, ch + 16, H), BF16), V((rows, ch + 16, H), BF16),
                V((rows, 3 * ch, H), BF16), V((rows, 3 * ch, H), BF16),
                V((rows, ch, H), BF16), V((rows, ch, H), BF16),
                V((ch + 16, H), BF16), V((cols, ch + 16, H), BF16),
                V((3 * ch, H), BF16), V((cols, 3 * ch, H), BF16),
                V((ch, H), BF16), V((cols, ch, H), BF16),
                V((rows, ch, H), BF16), V((rows, 3 * ch, H), BF16), V((rows, ch, H), BF16),
                dma((3,)), dma((4, NCH)), dma((4, NCH)),
                dma((cols,)), dma((cols,)), dma((cols,)), dma((cols,)),
                dma((3, rows)), dma((3, rows)), dma((3, cols)), dma((3, cols)),
                dma((3, rows)), dma((3, rows)),
            ],
            compiler_params=pltpu.CompilerParams(
                collective_id=0, has_side_effects=True, vmem_limit_bytes=60 * 1024 * 1024
            ),
        )(gate_count, tok_count, gate_feats[0, 0], adjacency[0, 0], membership[0, 0],
          w_msg, w_query, w_key, w_value, w_out, w_score[None], cotangent[0])
        return (outs[0][None], *outs[1:6], outs[6][0])

    placed = (
        P("row", "col", None, None),
        P("row", "col", None, None, None, None),
        P("row", "col"),
        P("row", "col", None, None),
        P("row", "col"),
        P(), P(), P(), P(), P(), P(),
        P("row", "col", None),
    )
    return jax.shard_map(
        body,
        mesh=mesh,
        in_specs=placed,
        out_specs=(P("row", "col", None), P(), P(), P(), P(), P(), P()),
        check_vma=False,
    )
```

```python
import math

import jax
import jax.numpy as jnp
from jax import lax
from jax.experimental import pallas as pl
from jax.experimental.pallas import tpu as pltpu
from jax.sharding import PartitionSpec as P

H = 256
HEADS = 2
HD = 128
BLK = 128
NB = 8
NT = 512
G = NB * BLK
NCH = 4
CG = G // NCH
EPS = 1e-06
F32 = jnp.float32
BF16 = jnp.bfloat16
MESH = pl.DeviceIdType.MESH


def mm(a, b):
    return jnp.dot(a, b, preferred_element_type=F32)


def mm_nt(a, b):
    return lax.dot_general(a, b, (((1,), (1,)), ((), ())), preferred_element_type=F32)


def mm_tn(a, b):
    return lax.dot_general(a, b, (((0,), (0,)), ((), ())), preferred_element_type=F32)


def remote(src, dst, send, recv, axis, peer):
    return pltpu.make_async_remote_copy(
        src_ref=src, dst_ref=dst, send_sem=send, recv_sem=recv,
        device_id={axis: peer}, device_id_type=MESH,
    )


def others(size, func):
    def step(s, carry):
        func(s)
        return carry

    lax.fori_loop(1, size, step, 0)


def rms_forward(values_in):
    rscale = lax.rsqrt(jnp.mean(values_in * values_in, axis=-1, keepdims=True) + EPS)
    return (values_in * rscale, rscale)


def rms_backward(grad_in, normed, rscale):
    return rscale * (grad_in - normed * jnp.mean(grad_in * normed, axis=-1, keepdims=True))


def prob_parts(scores):
    expo = math.log2(NT) - scores * (math.log2(math.e) / math.sqrt(HD))
    power = jnp.exp2(jnp.minimum(expo, 120.0))
    prob = pl.reciprocal(1.0 + power, approx=True)
    return prob, prob * (prob * power) * (1.0 / math.sqrt(HD))


def kernel(
    rows, cols,
    gate_count, tok_count, feats_hbm, adj_hbm, mem_hbm,
    w_msg, w_query, w_key, w_value, w_out, w_score, cot,
    value_out, g_score, out_a, out_b, out_c,
    feats, live, halo, adj_i, mem_i, adj, inv_deg, mem, mem_t, inv_cnt,
    message, preact, pooled, normed, rscale,
    tok, q_all, k_all, v_all, ga_all, d_own, p_t, d_t, att, gq, gk, gv, gmix,
    sa, ra, sb, rb, sc, rc, ta, ua, tb, ub, tc, uc, fa, fb, fc,
    local_sem, halo_s, halo_r, tok_s, tok_r, ga_s, ga_r,
    one_s, one_r, two_s, two_r, three_s, three_r,
):
    r = lax.axis_index("row")
    c = lax.axis_index("col")
    ch = H // rows

    load_feats = pltpu.make_async_copy(feats_hbm, feats, local_sem.at[0])
    load_adj = pltpu.make_async_copy(adj_hbm, adj_i, local_sem.at[1])
    load_mem = pltpu.make_async_copy(mem_hbm, mem_i, local_sem.at[2])
    load_feats.start()
    load_adj.start()
    load_mem.start()

    barrier = pltpu.get_barrier_semaphore()
    others(rows, lambda s: pl.semaphore_signal(
        barrier, inc=1, device_id={"row": lax.rem(r + s, rows)}, device_id_type=MESH))
    others(cols, lambda s: pl.semaphore_signal(
        barrier, inc=1, device_id={"col": lax.rem(c + s, cols)}, device_id_type=MESH))

    gates = gate_count[0, 0]
    load_feats.wait()
    for i in range(NCH):
        alive = (lax.broadcasted_iota(jnp.int32, (CG, 1), 0) + i * CG < gates).astype(F32)
        live[i] = (feats[i * CG:(i + 1) * CG].astype(F32) * alive).astype(BF16)
    pl.semaphore_wait(barrier, rows + cols - 2)

    ways = (
        (2, "col", 1, c < cols - 1, c > 0),
        (3, "col", -1, c > 0, c < cols - 1),
        (0, "row", 1, r < rows - 1, r > 0),
        (1, "row", -1, r > 0, r < rows - 1),
    )
    place = {"row": r, "col": c}

    def halo_copy(way, i):
        slot, axis, step, _, _ = way
        return remote(live.at[i], halo.at[slot, i], halo_s.at[slot, i], halo_r.at[slot, i],
                      axis, place[axis] + step)

    for way in ways:
        @pl.when(jnp.logical_not(way[4]))
        def _(way=way):
            halo[way[0]] = jnp.zeros((NCH, CG, H), BF16)

        @pl.when(way[3])
        def _(way=way):
            for i in range(NCH):
                halo_copy(way, i).start()

    load_adj.wait()

    def adj_step(b, carry):
        parts = [adj_i[b, k].astype(F32) for k in range(5)]
        total = parts[0] + parts[1] + parts[2] + parts[3] + parts[4]
        inv_deg[b] = 1.0 / (jnp.sum(total, axis=1, keepdims=True) + 1.0)
        for k in range(5):
            adj[b, :, k * BLK:(k + 1) * BLK] = parts[k].astype(BF16)
        return carry

    lax.fori_loop(0, NB, adj_step, 0)
    load_mem.wait()
    count = jnp.zeros((NT, 1), F32)
    for i in range(NCH):
        part = mem_i[:, i * CG:(i + 1) * CG].astype(F32)
        count = count + jnp.sum(part, axis=1, keepdims=True)
        mem[i] = part.astype(BF16)
        mem_t[i] = part.T.astype(BF16)
    inv_cnt[...] = 1.0 / (count + 1.0)

    pooled[...] = jnp.zeros((NT, H), F32)

    def gate_step(i, carry):
        for way in ways:
            @pl.when(way[4])
            def _(way=way):
                slot, axis, step, _, _ = way
                remote(live.at[i], halo.at[slot, i], halo_s.at[slot, i], halo_r.at[slot, i],
                       axis, place[axis] - step).wait_recv()
        own = live[i]
        for b in range(CG // BLK):
            cut = slice(b * BLK, (b + 1) * BLK)
            blk = i * (CG // BLK) + b
            srcs = jnp.concatenate([own[cut]] + [halo[k, i, cut] for k in range(4)], axis=0)
            message[i, cut] = (mm(adj[blk], srcs) * inv_deg[blk]).astype(BF16)
        pre = mm(message[i], w_msg[...])
        preact[i] = pre
        alive = (lax.broadcasted_iota(jnp.int32, (CG, 1), 0) + i * CG < gates).astype(F32)
        hidden = (alive * (own.astype(F32) + pre / (1.0 + jnp.exp(-pre)))).astype(BF16)
        pooled[...] += mm(mem[i], hidden)
        return carry

    lax.fori_loop(0, NCH, gate_step, 0)

    n_live = tok_count[0, 0]
    tlive = (lax.broadcasted_iota(jnp.int32, (NT, 1), 0) < n_live).astype(F32)
    norm_val, rs_val = rms_forward(pooled[...] * inv_cnt[...])
    normed[...] = norm_val
    rscale[...] = rs_val
    tok[c] = (tlive * norm_val).astype(BF16)

    own_tok = tok[c]
    half = NT // 2

    def chain_copy(buf, send, recv, src, k, step):
        part = buf.at[src, pl.ds(k * half, half)]
        return remote(part, part, send.at[src, k], recv.at[src, k], "col", c + step)

    def chain(buf, send, recv):
        def own(action):
            @pl.when(c < cols - 1)
            def _():
                for k in range(2):
                    action(chain_copy(buf, send.at[0], recv, c, k, 1))

            @pl.when(c > 0)
            def _():
                for k in range(2):
                    action(chain_copy(buf, send.at[1], recv, c, k, -1))

        def on(src, lane, step, more, wait):
            for k in range(2):
                if wait:
                    chain_copy(buf, send.at[lane], recv, src, k, -step).wait_recv()

                @pl.when(more)
                def _(k=k):
                    copy = chain_copy(buf, send.at[lane], recv, src, k, step)
                    copy.start() if wait else copy.wait_send()

        def hop(d, wait=True):
            @pl.when(c - d >= 0)
            def _():
                on(c - d, 0, 1, c < cols - 1, wait)

            @pl.when(c + d < cols)
            def _():
                on(c + d, 1, -1, c > 0, wait)

        return own, hop

    def at_distance(d, func):
        @pl.when(c - d >= 0)
        def _():
            func(c - d)

        @pl.when(c + d < cols)
        def _():
            func(c + d)

    tok_own, tok_hop = chain(tok, tok_s, tok_r)
    ga_own, ga_hop = chain(ga_all, ga_s, ga_r)
    tok_own(lambda copy: copy.start())

    q_all[c] = mm(own_tok, w_query[...]).astype(BF16)
    att[...] = jnp.zeros((NT, H), F32)

    def attend(src):
        k_all[src] = mm(tok[src], w_key[...]).astype(BF16)
        v_all[src] = mm(tok[src], w_value[...]).astype(BF16)
        for h in range(HEADS):
            lanes = slice(h * HD, (h + 1) * HD)
            prob, slope = prob_parts(mm_nt(q_all[c, :, lanes], k_all[src, :, lanes]))
            d_own[src, h] = slope.astype(BF16)
            att[:, lanes] += mm(prob.astype(BF16), v_all[src, :, lanes])

    def key_probs(src):
        for h in range(HEADS):
            lanes = slice(h * HD, (h + 1) * HD)
            prob, slope = prob_parts(mm_nt(k_all[c, :, lanes], q_all[src, :, lanes]))
            p_t[src, h] = prob.astype(BF16)
            d_t[src, h] = slope.astype(BF16)

    def key_probs_of(src):
        q_all[src] = mm(tok[src], w_query[...]).astype(BF16)
        key_probs(src)

    attend(c)
    key_probs(c)

    def attend_step(d, carry):
        tok_hop(d)
        at_distance(d, attend)

        @pl.when(d < cols - 1)
        def _():
            at_distance(d, key_probs_of)

        return carry

    lax.fori_loop(1, cols, attend_step, 0)

    attended = att[...].astype(BF16)
    pnormed, pscale = rms_forward(mm(attended, w_out[...]))
    mixed = own_tok.astype(F32) + pnormed
    score_w = w_score[...].astype(F32)
    val = tlive * jnp.sum(mixed * score_w, axis=1, keepdims=True)
    value_out[...] = jnp.broadcast_to(val, (NT, 128)).T[0:1]
    cot_col = jnp.broadcast_to(cot[...], (128, NT)).T[:, 0:1]
    grad_value = tlive * cot_col * (1.0 / math.sqrt(rows * cols * NT))
    grad_mixed = grad_value * score_w
    gmix[...] = grad_mixed
    grad_proj = rms_backward(grad_mixed, pnormed, pscale).astype(BF16)
    ga_all[c] = mm_nt(grad_proj, w_out[...]).astype(BF16)

    ga_own(lambda copy: copy.start())

    def one_copy(g, send, recv, peer, slot):
        return remote(send.at[peer], recv.at[slot], one_s.at[g, peer], one_r.at[g, slot], "row", peer)

    def one_start(g, send, recv):
        recv[r] = send[r]
        others(rows, lambda s: one_copy(g, send, recv, lax.rem(r + s, rows), r).start())

    def two_copy(g, send, recv, peer, slot):
        return remote(send, recv.at[slot], two_s.at[g, peer], two_r.at[g, slot], "col", peer)

    def two_start(g, send, recv, mid, gathered):
        others(rows, lambda s: one_copy(
            g, send, recv, lax.rem(r + s, rows), lax.rem(r + s, rows)).wait_recv())
        total = recv[0].astype(F32)
        for p in range(1, rows):
            total = total + recv[p].astype(F32)
        mid[...] = total.astype(BF16)
        gathered[c] = mid[...]
        others(cols, lambda s: two_copy(g, mid, gathered, lax.rem(c + s, cols), c).start())

    def three_copy(g, full, peer, slot):
        return remote(full.at[slot], full.at[slot], three_s.at[g, peer], three_r.at[g, slot],
                      "row", peer)

    def three_start(g, mid, gathered, full, span):
        others(cols, lambda s: two_copy(
            g, mid, gathered, lax.rem(c + s, cols), lax.rem(c + s, cols)).wait_recv())
        total = gathered[0].astype(F32)
        for p in range(1, cols):
            total = total + gathered[p].astype(F32)
        full[r] = total[:span].astype(BF16)
        others(rows, lambda s: three_copy(g, full, lax.rem(r + s, rows), r).start())
        return total

    def three_wait(g, full):
        others(rows, lambda s: three_copy(
            g, full, lax.rem(r + s, rows), lax.rem(r + s, rows)).wait_recv())

    def finish(g, send, recv, mid, gathered, full):
        def row_send(s):
            p = lax.rem(r + s, rows)
            one_copy(g, send, recv, p, r).wait_send()
            three_copy(g, full, p, r).wait_send()

        others(rows, row_send)
        others(cols, lambda s: two_copy(g, mid, gathered, lax.rem(c + s, cols), c).wait_send())

    score_part = jnp.broadcast_to(jnp.sum(mixed * grad_value, axis=0, keepdims=True), (16, H))
    out_part = mm_tn(attended, grad_proj)
    for p in range(rows):
        sa[p, 0:ch] = out_part[p * ch:(p + 1) * ch].astype(BF16)
        sa[p, 2 * ch:2 * ch + 16] = score_part.astype(BF16)

    gq[...] = jnp.zeros((NT, H), F32)
    gk[...] = jnp.zeros((NT, H), F32)
    gv[...] = jnp.zeros((NT, H), F32)

    def query_step(src, carry):
        for h in range(HEADS):
            lanes = slice(h * HD, (h + 1) * HD)
            grad_prob = mm_nt(ga_all[c, :, lanes], v_all[src, :, lanes])
            grad_score = (grad_prob * d_own[src, h].astype(F32)).astype(BF16)
            gq[:, lanes] += mm(grad_score, k_all[src, :, lanes])
        return carry

    lax.fori_loop(0, cols, query_step, 0)
    grad_query = gq[...].astype(BF16)
    part = mm_tn(own_tok, grad_query).astype(BF16)
    for p in range(rows):
        sa[p, ch:2 * ch] = part[p * ch:(p + 1) * ch]
    one_start(0, sa, ra)

    def key_grads(src):
        for h in range(HEADS):
            lanes = slice(h * HD, (h + 1) * HD)
            grad_prob = mm_nt(v_all[c, :, lanes], ga_all[src, :, lanes])
            grad_score = (grad_prob * d_t[src, h].astype(F32)).astype(BF16)
            gk[:, lanes] += mm(grad_score, q_all[src, :, lanes])
            gv[:, lanes] += mm(p_t[src, h], ga_all[src, :, lanes])

    def key_step(d, carry):
        ga_hop(d)
        at_distance(d, key_grads)
        return carry

    ga_hop(1)
    at_distance(cols - 1, key_probs_of)
    key_grads(c)
    at_distance(1, key_grads)
    two_start(0, sa, ra, ta, ua)
    gmix[...] += mm_nt(grad_query, w_query[...])
    lax.fori_loop(2, cols, key_step, 0)

    grad_key = gk[...].astype(BF16)
    grad_val = gv[...].astype(BF16)
    for j, grad in enumerate((grad_key, grad_val)):
        part = mm_tn(own_tok, grad).astype(BF16)
        for p in range(rows):
            sb[p, j * ch:(j + 1) * ch] = part[p * ch:(p + 1) * ch]
    one_start(1, sb, rb)

    grad_tokens = gmix[...] + mm_nt(grad_key, w_key[...])
    grad_tokens = grad_tokens + mm_nt(grad_val, w_value[...])
    grad_pooled = rms_backward(tlive * grad_tokens, normed[...], rscale[...])
    grad_scaled = (grad_pooled * inv_cnt[...]).astype(BF16)
    total = three_start(0, ta, ua, fa, 2 * ch)
    g_score[...] = total[2 * ch:2 * ch + 1]
    msg_part = jnp.zeros((H, H), F32)
    for i in range(NCH):
        alive = (lax.broadcasted_iota(jnp.int32, (CG, 1), 0) + i * CG < gates).astype(F32)
        pre = preact[i]
        sig = 1.0 / (1.0 + jnp.exp(-pre))
        grad_pre = alive * mm(mem_t[i], grad_scaled) * (sig * (1.0 + pre * (1.0 - sig)))
        msg_part = msg_part + mm_tn(message[i], grad_pre.astype(BF16))
    for p in range(rows):
        sc[p] = msg_part[p * ch:(p + 1) * ch].astype(BF16)
    one_start(2, sc, rc)
    two_start(1, sb, rb, tb, ub)
    two_start(2, sc, rc, tc, uc)
    three_start(1, tb, ub, fb, 2 * ch)
    three_start(2, tc, uc, fc, ch)
    three_wait(0, fa)
    out_a[...] = fa[...]
    three_wait(1, fb)
    out_b[...] = fb[...]
    three_wait(2, fc)
    out_c[...] = fc[...]

    for way in ways:
        @pl.when(way[3])
        def _(way=way):
            for i in range(NCH):
                halo_copy(way, i).wait_send()

    tok_own(lambda copy: copy.wait_send())
    ga_own(lambda copy: copy.wait_send())

    def sent(d, carry):
        tok_hop(d, False)
        ga_hop(d, False)
        return carry

    lax.fori_loop(1, cols, sent, 0)
    finish(0, sa, ra, ta, ua, fa)
    finish(1, sb, rb, tb, ub, fb)
    finish(2, sc, rc, tc, uc, fc)


def unpack(rows, value_in, score_in, in_a, in_b, in_c,
           value_out, g_msg, g_query, g_key, g_value, g_out, g_score):
    ch = H // rows
    value_out[0] = value_in[...]
    g_score[...] = score_in[...]
    for p in range(rows):
        cut = slice(p * ch, (p + 1) * ch)
        g_out[cut] = in_a[p, 0:ch].astype(F32)
        g_query[cut] = in_a[p, ch:2 * ch].astype(F32)
        g_key[cut] = in_b[p, 0:ch].astype(F32)
        g_value[cut] = in_b[p, ch:2 * ch].astype(F32)
        g_msg[cut] = in_c[p].astype(F32)


def solution(mesh):
    rows, cols = mesh.shape["row"], mesh.shape["col"]
    ch = H // rows

    def body(gate_feats, adjacency, gate_count, membership, tok_count,
             w_msg, w_query, w_key, w_value, w_out, w_score, cotangent):
        vmem = pl.BlockSpec(memory_space=pltpu.VMEM)
        smem = pl.BlockSpec(memory_space=pltpu.SMEM)
        hbm = pl.BlockSpec(memory_space=pl.ANY)
        wide = jax.ShapeDtypeStruct((H, H), F32)
        dma = pltpu.SemaphoreType.DMA
        V = pltpu.VMEM
        outs = pl.pallas_call(
            lambda *refs: kernel(rows, cols, *refs),
            out_shape=[jax.ShapeDtypeStruct((1, NT), F32), jax.ShapeDtypeStruct((1, H), F32)]
            + [jax.ShapeDtypeStruct((rows, n * ch, H), BF16) for n in (2, 2, 1)],
            in_specs=[smem, smem, hbm, hbm, hbm] + [vmem] * 7,
            out_specs=[vmem] * 5,
            scratch_shapes=[
                V((G, H), BF16), V((NCH, CG, H), BF16), V((4, NCH, CG, H), BF16),
                V((NB, 5, BLK, BLK), jnp.int32), V((NT, G), jnp.int32),
                V((NB, BLK, 5 * BLK), BF16), V((NB, BLK, 1), F32),
                V((NCH, NT, CG), BF16), V((NCH, CG, NT), BF16), V((NT, 1), F32),
                V((NCH, CG, H), BF16), V((NCH, CG, H), F32), V((NT, H), F32),
                V((NT, H), F32), V((NT, 1), F32),
                V((cols, NT, H), BF16), V((cols, NT, H), BF16), V((cols, NT, H), BF16),
                V((cols, NT, H), BF16), V((cols, NT, H), BF16),
                V((cols, HEADS, NT, NT), BF16), V((cols, HEADS, NT, NT), BF16),
                V((cols, HEADS, NT, NT), BF16),
                V((NT, H), F32), V((NT, H), F32), V((NT, H), F32), V((NT, H), F32),
                V((NT, H), F32),
                V((rows, 2 * ch + 16, H), BF16), V((rows, 2 * ch + 16, H), BF16),
                V((rows, 2 * ch, H), BF16), V((rows, 2 * ch, H), BF16),
                V((rows, ch, H), BF16), V((rows, ch, H), BF16),
                V((2 * ch + 16, H), BF16), V((cols, 2 * ch + 16, H), BF16),
                V((2 * ch, H), BF16), V((cols, 2 * ch, H), BF16),
                V((ch, H), BF16), V((cols, ch, H), BF16),
                V((rows, 2 * ch, H), BF16), V((rows, 2 * ch, H), BF16), V((rows, ch, H), BF16),
                dma((3,)), dma((4, NCH)), dma((4, NCH)),
                dma((2, cols, 2)), dma((cols, 2)), dma((2, cols, 2)), dma((cols, 2)),
                dma((3, rows)), dma((3, rows)), dma((3, cols)), dma((3, cols)),
                dma((3, rows)), dma((3, rows)),
            ],
            compiler_params=pltpu.CompilerParams(
                collective_id=0, has_side_effects=True, vmem_limit_bytes=60 * 1024 * 1024
            ),
        )(gate_count, tok_count, gate_feats[0, 0], adjacency[0, 0], membership[0, 0],
          w_msg, w_query, w_key, w_value, w_out, w_score[None], cotangent[0])
        done = pl.pallas_call(
            lambda *refs: unpack(rows, *refs),
            out_shape=[jax.ShapeDtypeStruct((1, 1, NT), F32), wide, wide, wide, wide, wide,
                       jax.ShapeDtypeStruct((1, H), F32)],
            in_specs=[vmem] * 5,
            out_specs=[vmem] * 7,
        )(*outs)
        return (*done[:6], done[6][0])

    placed = (
        P("row", "col", None, None),
        P("row", "col", None, None, None, None),
        P("row", "col"),
        P("row", "col", None, None),
        P("row", "col"),
        P(), P(), P(), P(), P(), P(),
        P("row", "col", None),
    )
    return jax.shard_map(
        body,
        mesh=mesh,
        in_specs=placed,
        out_specs=(P("row", "col", None), P(), P(), P(), P(), P(), P()),
        check_vma=False,
    )
```
